256 devices in a mesh: row: 16 (over y, z_hi), col: 16 (over z_lo, x, core).
Axes of the slice: x: 4, y: 4, z: 8 (z_hi: 4, z_lo: 2; z = z_hi * 2 + z_lo), core: 2. Of those that a mesh axis runs over, the one named last changes fastest.
Arguments:
- pair: bfloat16 [2048, 2048, 128], P('row', 'col'), may hold values from -6 to 6
- pair_mask: int32 [2048, 2048], P('row', 'col'), may hold values 0 or 1
- in_gain: float32 [2, 128], replicated, may hold values from 0.1 to 1.9
- in_bias: float32 [2, 128], replicated, may hold values from -2 to 2
- proj_weight: bfloat16 [2, 128, 512], replicated, may hold values from -0.5 to 0.5
- gate_weight: bfloat16 [2, 128, 128], replicated, may hold values from -0.5 to 0.5
- out_gain: float32 [2, 128], replicated, may hold values from 0.1 to 1.9
- out_bias: float32 [2, 128], replicated, may hold values from -2 to 2
- out_weight: bfloat16 [2, 128, 128], replicated, may hold values from -0.5 to 0.5
Outputs:
- updated: bfloat16 [2048, 2048, 128], P('row', 'col')
The draws below stay inside these ranges and needn't reach their ends.
All inputs are finite; a program needn't handle non-finite values. No bound on the sum of `pair_mask` on one device may be relied on, other than what follows from the above.
Results may differ from the reference program's by a relative error of at most 0.015.
Values may be sent and summed in bfloat16 or wider, within the bound.
A program may use at most 128 MiB of HBM per device.

```python
import jax
import jax.numpy as jnp
from jax import lax

C = 128
TOKENS = 2048
WIN_DEV = 8
ROWS_DEV = 128
COLS_DEV = 128
WIN_OUT = 128
WIN_IN = 128
N_ROW = 16
N_COL = 16


def touch_ends(entries, stream_key, low, top_value):
    dims = entries.shape
    index_at = [jax.random.randint(jax.random.fold_in(stream_key, axis), (), 0, dims[axis]) for axis in range(len(dims))]
    entries = entries.at[tuple(index_at)].set(low)
    longest = dims.index(max(dims))
    index_at[longest] = (index_at[longest] + 1) % dims[longest]
    return entries.at[tuple(index_at)].set(top_value)


def levels(key, extent, shards, smallest, high):
    def one(axis_at, blocks):
        heights = jax.random.uniform(jax.random.fold_in(jax.random.fold_in(key, 6), axis_at), (blocks,), jnp.float32, smallest / len(shards), high / len(shards))
        return jnp.repeat(jnp.exp(heights), extent[axis_at] // blocks).reshape((-1,) + (1,) * (len(extent) - axis_at - 1))

    factor_of = one(*shards[0])
    for cut in shards[1:]:
        factor_of = factor_of * one(*cut)
    return factor_of


def gaussian(key, dims, deviation, limit, shards=(), held_as=jnp.bfloat16):
    factor_of = levels(key, dims, shards, -0.22, 0.18) if shards else 1.0
    entries = jax.random.normal(key, dims, jnp.float32) * deviation * factor_of
    return jnp.minimum(jnp.maximum(entries, -limit), limit).astype(held_as)


def setup_inputs(seed: int = 0) -> dict:
    keys = jax.random.split(jax.random.key(seed), 10)
    pair = gaussian(keys[0], (TOKENS, TOKENS, C), 1.0, 6.0, ((0, 16), (1, 16)))
    pair_mask = touch_ends((jax.random.randint(keys[1], (TOKENS, TOKENS), 0, 8) < 7).astype(jnp.int32), jax.random.fold_in(keys[1], 1), 0, 1)
    in_gain = jnp.clip(1.0 + 0.18 * jax.random.normal(keys[2], (2, C), jnp.float32), 0.1, 1.9)
    in_bias = gaussian(keys[3], (2, C), 0.4, 2.0, (), jnp.float32)
    proj_weight = gaussian(keys[4], (2, C, 4 * C), C ** -0.5, 0.5)
    gate_weight = gaussian(keys[5], (2, C, C), C ** -0.5, 0.5)
    out_gain = jnp.clip(1.0 + 0.18 * jax.random.normal(keys[6], (2, C), jnp.float32), 0.1, 1.9)
    out_bias = gaussian(keys[7], (2, C), 0.4, 2.0, (), jnp.float32)
    out_weight = gaussian(keys[8], (2, C, C), C ** -0.5, 0.5)
    return {"pair": pair, "pair_mask": pair_mask, "in_gain": in_gain, "in_bias": in_bias, "proj_weight": proj_weight, "gate_weight": gate_weight, "out_gain": out_gain, "out_bias": out_bias, "out_weight": out_weight}


epsilon = 1e-05

def normalize(values, gain, bias_in):
    centre = lax.optimization_barrier(jnp.mean(values, -1, keepdims=True))
    shifted = values - centre
    variance = lax.optimization_barrier(jnp.mean(shifted * shifted, -1, keepdims=True))
    return shifted * lax.rsqrt(variance + epsilon) * gain + bias_in

def project(normed, window_mask, weight):
    channels = weight.shape[0]
    leading = normed.shape[:-1]
    projected = jnp.dot(normed.reshape(-1, channels), weight, preferred_element_type=jnp.float32)
    projected = projected.reshape(leading + (4 * channels,))
    keep_mask = window_mask.astype(jnp.float32)[..., None]
    first = keep_mask * jax.nn.sigmoid(projected[..., :channels]) * projected[..., channels:2 * channels]
    second = keep_mask * jax.nn.sigmoid(projected[..., 2 * channels:3 * channels]) * projected[..., 3 * channels:]
    return (first.astype(jnp.bfloat16), second.astype(jnp.bfloat16))

def finish(pair_block, summed, gain_in, bias_in, gate_w, gain_out, bias_out, out_w):
    channels = gate_w.shape[0]
    wide = pair_block.astype(jnp.float32)
    normed = normalize(wide, gain_in, bias_in).astype(jnp.bfloat16)
    gating = jax.nn.sigmoid(jnp.dot(normed.reshape(-1, channels), gate_w, preferred_element_type=jnp.float32))
    scaled = normalize(summed, gain_out, bias_out).astype(jnp.bfloat16)
    update = jnp.dot(scaled.reshape(-1, channels), out_w, preferred_element_type=jnp.float32)
    return (wide.reshape(-1, channels) + gating * update).reshape(pair_block.shape).astype(jnp.bfloat16)

def reference(pair, pair_mask, in_gain, in_bias, proj_weight, gate_weight, out_gain, out_bias, out_weight):
    block_rows = min(128, TOKENS)
    blocks = TOKENS // block_rows
    window = pair.reshape(TOKENS, N_COL, COLS_DEV, C)[:, :, :WIN_DEV].reshape(TOKENS, WIN_OUT, C)
    window_mask = pair_mask.reshape(TOKENS, N_COL, COLS_DEV)[:, :, :WIN_DEV].reshape(TOKENS, WIN_OUT)
    normed = normalize(window.astype(jnp.float32), in_gain[0], in_bias[0]).astype(jnp.bfloat16)
    left_side, right_side = project(normed, window_mask, proj_weight[0])
    right_wide = right_side.astype(jnp.float32)

    def out_rows(inputs):
        pair_block, panels = inputs
        summed = jnp.einsum('ikc,jkc->ijc', panels.astype(jnp.float32), right_wide)
        return finish(pair_block, summed, in_gain[0], in_bias[0], gate_weight[0], out_gain[0], out_bias[0], out_weight[0])
    middle = lax.map(out_rows, (pair.reshape(blocks, block_rows, TOKENS, C), left_side.reshape(blocks, block_rows, WIN_OUT, C)))
    middle = middle.reshape(TOKENS, TOKENS, C)
    window = middle.reshape(N_ROW, ROWS_DEV, TOKENS, C)[:, :WIN_DEV].reshape(WIN_IN, TOKENS, C)
    window_mask = pair_mask.reshape(N_ROW, ROWS_DEV, TOKENS)[:, :WIN_DEV].reshape(WIN_IN, TOKENS)
    normed = normalize(window.astype(jnp.float32), in_gain[1], in_bias[1]).astype(jnp.bfloat16)
    left_side, right_side = project(normed, window_mask, proj_weight[1])
    right_wide = right_side.astype(jnp.float32)
    left_blocks = left_side.reshape(WIN_IN, blocks, block_rows, C).transpose(1, 0, 2, 3)

    def in_rows(inputs):
        pair_block, panels = inputs
        summed = jnp.einsum('kic,kjc->ijc', panels.astype(jnp.float32), right_wide)
        return finish(pair_block, summed, in_gain[1], in_bias[1], gate_weight[1], out_gain[1], out_bias[1], out_weight[1])
    result = lax.map(in_rows, (middle.reshape(blocks, block_rows, TOKENS, C), left_blocks))
    return result.reshape(TOKENS, TOKENS, C)
```

```python
import jax
import jax.numpy as jnp
from jax import lax
from jax.sharding import PartitionSpec as P

WIN_DEV = 8


epsilon = 1e-05


def swap_axes(value):
    size = lax.axis_size("row")
    pairs = [(r * size + c, c * size + r) for r in range(size) for c in range(size)]
    return lax.ppermute(value, ("row", "col"), pairs)


def normalize(values, gain, bias_in):
    centre = jnp.mean(values, -1, keepdims=True)
    shifted = values - centre
    variance = jnp.mean(shifted * shifted, -1, keepdims=True)
    return shifted * lax.rsqrt(variance + epsilon) * gain + bias_in


def project(normed, window_mask, weight):
    channels = weight.shape[0]
    leading = normed.shape[:-1]
    projected = jnp.dot(normed.reshape(-1, channels), weight, preferred_element_type=jnp.float32)
    projected = projected.reshape(leading + (4 * channels,))
    keep_mask = window_mask.astype(jnp.float32)[..., None]
    first = (
        keep_mask
        * jax.nn.sigmoid(projected[..., :channels])
        * projected[..., channels : 2 * channels]
    )
    second = (
        keep_mask
        * jax.nn.sigmoid(projected[..., 2 * channels : 3 * channels])
        * projected[..., 3 * channels :]
    )
    return (first.astype(jnp.bfloat16), second.astype(jnp.bfloat16))


def finish(pair_block, normed, summed, gate_w, gain_out, bias_out, out_w):
    channels = gate_w.shape[0]
    gating = jax.nn.sigmoid(
        jnp.dot(normed.reshape(-1, channels), gate_w, preferred_element_type=jnp.float32)
    )
    scaled = normalize(summed, gain_out, bias_out).astype(jnp.bfloat16)
    update = jnp.dot(scaled.reshape(-1, channels), out_w, preferred_element_type=jnp.float32)
    wide = pair_block.astype(jnp.float32).reshape(-1, channels)
    return (wide + gating * update).reshape(pair_block.shape).astype(jnp.bfloat16)


def per_device(
    pair, pair_mask, in_gain, in_bias, proj_weight, gate_weight, out_gain, out_bias, out_weight
):
    normed = normalize(pair.astype(jnp.float32), in_gain[0], in_bias[0]).astype(jnp.bfloat16)
    left_own, right_own = project(normed[:, :WIN_DEV], pair_mask[:, :WIN_DEV], proj_weight[0])
    swapped = swap_axes(right_own)
    left_side = lax.all_gather(left_own, "col", axis=1, tiled=True)
    right_side = lax.all_gather(swapped, "row", axis=1, tiled=True)
    summed = jnp.einsum("ikc,jkc->ijc", left_side, right_side, preferred_element_type=jnp.float32)
    middle = finish(pair, normed, summed, gate_weight[0], out_gain[0], out_bias[0], out_weight[0])
    normed = normalize(middle.astype(jnp.float32), in_gain[1], in_bias[1]).astype(jnp.bfloat16)
    left_own, right_own = project(normed[:WIN_DEV], pair_mask[:WIN_DEV], proj_weight[1])
    swapped = swap_axes(left_own)
    right_side = lax.all_gather(right_own, "row", axis=0, tiled=True)
    left_side = lax.all_gather(swapped, "col", axis=0, tiled=True)
    summed = jnp.einsum("kic,kjc->ijc", left_side, right_side, preferred_element_type=jnp.float32)
    return finish(middle, normed, summed, gate_weight[1], out_gain[1], out_bias[1], out_weight[1])


def solution(mesh):
    placed = (P("row", "col", None), P("row", "col"), P(), P(), P(), P(), P(), P(), P())
    return jax.shard_map(
        per_device, mesh=mesh, in_specs=placed, out_specs=P("row", "col", None), check_vma=False
    )
```

```python
import functools

import jax
import jax.numpy as jnp
from jax import lax
from jax.experimental import pallas as pl
from jax.experimental.pallas import tpu as pltpu
from jax.sharding import PartitionSpec as P

C = 128
N = 128
WIN = 8
RING = 16
PIECE = C * WIN
HALF = PIECE // 2
EPS = 1e-5
MIB = 1024 * 1024
SEMS = 160
F32 = jnp.float32
BF16 = jnp.bfloat16


def xor(a, b):
    total = 0
    for bit in (1, 2, 4, 8):
        total = total + lax.rem(lax.div(a, bit) + lax.div(b, bit), 2) * bit
    return total


def sigmoid(z):
    return 0.5 * jnp.tanh(0.5 * z) + 0.5


def norm_lanes(x, gain, bias):
    centre = jnp.mean(x, -1, keepdims=True)
    s = x - centre
    var = jnp.mean(s * s, -1, keepdims=True)
    return s * lax.rsqrt(var + EPS) * gain + bias


def kernel(
    pair_ref, mask_ref, ing_ref, inb_ref, pw_ref, gw_ref, outg_ref, outb_ref, ow_ref, out_ref,
    wbuf, pairv, gate, a1, b1, a2, b2, xs, ha, hb, hat, hbt, own, mid_sw, parity, cols, maskt,
    ssem, rsem, lsem,
):
    r = lax.axis_index("row")
    c = lax.axis_index("col")
    y, zh = lax.div(r, 4), lax.rem(r, 4)
    zl, x, core = lax.div(c, 8), lax.rem(lax.div(c, 2), 4), lax.rem(c, 2)
    rc = xor(r, c)

    def row_at(dz, dy):
        return lax.rem(y + dy + 4, 4) * 4 + lax.rem(zh + dz + 4, 4)

    def col_at(dl, dx):
        return lax.rem(zl + dl, 2) * 8 + lax.rem(x + dx + 4, 4) * 2 + core

    sibling = c + 1 - 2 * core

    load_w = pltpu.make_async_copy(pair_ref.at[:, pl.ds(0, 16), :], wbuf, lsem.at[0])
    load_w.start()
    load_p = pltpu.make_async_copy(pair_ref, pairv, lsem.at[1])
    load_p.start()

    bar = pltpu.get_barrier_semaphore()

    def greet(dev):
        pl.semaphore_signal(bar, inc=1, device_id=dev, device_id_type=pl.DeviceIdType.MESH)

    fixed = [
        (row_at(0, 1), c), (row_at(0, -1), c), (row_at(1, 0), c), (row_at(-1, 0), c),
        (r, col_at(0, 1)), (r, col_at(0, -1)), (r, col_at(1, 0)), (r, sibling),
    ]
    for dev in fixed:
        greet(dev)

    @pl.when(c != 0)
    def _():
        greet((rc, c))

    @pl.when(r != 0)
    def _():
        greet((r, rc))

    copies = {}

    def make(name, src, dst, dev):
        n = len(copies)
        cp = pltpu.make_async_remote_copy(
            src_ref=src, dst_ref=dst, send_sem=ssem.at[n], recv_sem=rsem.at[n],
            device_id=dev, device_id_type=pl.DeviceIdType.MESH,
        )
        copies[name] = cp
        return cp

    def post(name, src, dst, dev):
        make(name, src, dst, dev).start()

    def got(name):
        copies[name].wait_recv()

    def half(ref, slot, h):
        return ref.at[slot, pl.ds(h * HALF, HALF), :]

    def prepare():
        row = lax.broadcasted_iota(jnp.int32, (256, N), 0)
        low = lax.rem(row, 16) < 8
        parity[0] = jnp.where(low, 1.0, 0.0).astype(BF16)
        parity[1] = jnp.where(low, 0.0, 1.0).astype(BF16)
        for d in range(2):
            cols[2 * d] = jnp.broadcast_to(outg_ref[pl.ds(d, 1), :], (C, C)).T
            cols[2 * d + 1] = jnp.broadcast_to(outb_ref[pl.ds(d, 1), :], (C, C)).T
        maskt[...] = mask_ref[...].astype(F32).T

    def project(n, d, store):
        h = jnp.dot(n, pw_ref[d], preferred_element_type=F32)
        store(ha, sigmoid(h[:, :C]) * h[:, C : 2 * C])
        store(hb, sigmoid(h[:, 2 * C : 3 * C]) * h[:, 3 * C :])

    def window_out():
        g, b = ing_ref[pl.ds(0, 1), :], inb_ref[pl.ds(0, 1), :]

        def body(t, carry):
            v = wbuf[pl.ds(t * 16, 16)].astype(F32)[:, :WIN, :].reshape(16 * WIN, C)
            n = norm_lanes(v, g, b).astype(BF16)

            def store(ref, val):
                ref[pl.ds(pl.multiple_of(t * 128, 128), 128), :] = val

            project(n, 0, store)
            return carry

        lax.fori_loop(0, 8, body, 0)
        for src, dst in ((ha, hat), (hb, hbt)):
            for k in range(WIN):
                t = src[pl.ds(k, N, stride=WIN), :].T
                dst[pl.ds(k, C, stride=WIN), :] = t * maskt[pl.ds(k, 1), :]

    def window_in():
        g, b = ing_ref[pl.ds(1, 1), :], inb_ref[pl.ds(1, 1), :]
        for k in range(WIN):
            v = pairv[k].astype(F32)
            n = norm_lanes(v, g, b).astype(BF16)
            m = mask_ref[pl.ds(k, 1), :].astype(F32)
            h = jnp.dot(n, pw_ref[1], preferred_element_type=F32)
            av = sigmoid(h[:, :C]) * h[:, C : 2 * C]
            bv = sigmoid(h[:, 2 * C : 3 * C]) * h[:, 3 * C :]
            hat[pl.ds(k, C, stride=WIN), :] = av.T * m
            hbt[pl.ds(k, C, stride=WIN), :] = bv.T * m

    def gate_rows(lo, hi, d):
        g, b = ing_ref[pl.ds(d, 1), :], inb_ref[pl.ds(d, 1), :]

        def body(t, carry):
            v = pairv[pl.ds(t * 2, 2)].astype(F32).reshape(2 * N, C)
            n = norm_lanes(v, g, b).astype(BF16)
            z = jnp.dot(n, gw_ref[d], preferred_element_type=F32)
            gate[pl.ds(t * 2, 2)] = sigmoid(z).astype(BF16).reshape(2, N, C)
            return carry

        lax.fori_loop(lo // 2, hi // 2, body, 0)

    def product(a, b, lo, hi):
        def body(t, carry):
            rows = pl.ds(pl.multiple_of(t * 16, 16), 16)
            lhs = a[:, rows, :].reshape(256, N)
            rhs = b[:, rows, :].reshape(256, N)
            both = jnp.concatenate([rhs * parity[0], rhs * parity[1]], axis=1)
            out = lax.dot_general(lhs, both, (((0,), (0,)), ((), ())), preferred_element_type=F32)
            base = pl.multiple_of(t * 16, 16)
            xs[:, pl.ds(base, 8), :] = out[:, :N].reshape(16, 8, N)
            xs[:, pl.ds(base + 8, 8), :] = out[:, N:].reshape(16, 8, N)
            return carry

        lax.fori_loop(lo, hi, body, 0)

    def finish(lo, hi, d):
        def body(t, carry):
            for i8 in range(8):
                v = xs[t, pl.ds(i8, C, stride=8), :]
                centre = jnp.mean(v, 0, keepdims=True)
                s = v - centre
                var = jnp.mean(s * s, 0, keepdims=True)
                n = s * lax.rsqrt(var + EPS) * cols[2 * d] + cols[2 * d + 1]
                u = lax.dot_general(
                    n.astype(BF16), ow_ref[d], (((0,), (0,)), ((), ())), preferred_element_type=F32
                )
                i = t * 8 + i8
                old = pairv[i].astype(F32)
                pairv[i] = (old + gate[i].astype(F32) * u).astype(BF16)
            return carry

        lax.fori_loop(lo, hi, body, 0)

    def gather_steps(p, a, b, lab_a, lab_b):
        steps = []

        def b_first(h):
            s = half(b, lab_b(r), h)
            for dz in (1, -1):
                post((p, "z", dz, h), s, s, (row_at(dz, 0), c))
            for dy in (1, -1):
                post((p, "y", 0, dy, h), s, s, (row_at(0, dy), c))

        def b_z(dz, h):
            got((p, "z", dz, h))
            s = half(b, lab_b(row_at(-dz, 0)), h)
            if (dz == 1) == (h == 0):
                post((p, "z", 2, h), s, s, (row_at(dz, 0), c))
            for dy in (1, -1):
                post((p, "y", -dz, dy, h), s, s, (row_at(0, dy), c))

        def b_z2(h):
            got((p, "z", 2, h))
            s = half(b, lab_b(row_at(2, 0)), h)
            for dy in (1, -1):
                post((p, "y", 2, dy, h), s, s, (row_at(0, dy), c))

        def b_y(q, dy, h):
            got((p, "y", q, dy, h))
            if (dy == 1) == (h == 0):
                s = half(b, lab_b(row_at(q, -dy)), h)
                post((p, "y2", q, h), s, s, (row_at(0, dy), c))

        def b_y2(q, h):
            got((p, "y2", q, h))

        def a_first(h):
            s = half(a, lab_a(c), h)
            post((p, "l", h), s, s, (r, col_at(1, 0)))
            for dx in (1, -1):
                post((p, "x", 0, dx, h), s, s, (r, col_at(0, dx)))
            post((p, "k", 0, 0, h), s, s, (r, sibling))

        def a_l(h):
            got((p, "l", h))
            s = half(a, lab_a(col_at(1, 0)), h)
            for dx in (1, -1):
                post((p, "x", 1, dx, h), s, s, (r, col_at(0, dx)))
            post((p, "k", 1, 0, h), s, s, (r, sibling))

        def a_x(q, dx, h):
            got((p, "x", q, dx, h))
            s = half(a, lab_a(col_at(q, -dx)), h)
            if (dx == 1) == (h == 0):
                post((p, "x2", q, h), s, s, (r, col_at(0, dx)))
            post((p, "k", q, -dx, h), s, s, (r, sibling))

        def a_x2(q, h):
            got((p, "x2", q, h))
            s = half(a, lab_a(col_at(q, 2)), h)
            post((p, "k", q, 2, h), s, s, (r, sibling))

        def a_k():
            for q in (0, 1):
                for dx in (0, 1, -1, 2):
                    for h in (0, 1):
                        got((p, "k", q, dx, h))

        f = functools.partial
        bs = [f(b_z, 1, 0), f(b_z, -1, 0), f(b_z, 1, 1), f(b_z, -1, 1), f(b_z2, 0), f(b_z2, 1)]
        for q in (0, 1, -1, 2):
            for h in (0, 1):
                bs += [f(b_y, q, 1, h), f(b_y, q, -1, h)]
        for q in (0, 1, -1, 2):
            bs += [f(b_y2, q, 0), f(b_y2, q, 1)]
        as_ = [f(a_l, 0), f(a_l, 1)]
        for q in (0, 1):
            for h in (0, 1):
                as_ += [f(a_x, q, 1, h), f(a_x, q, -1, h)]
        for q in (0, 1):
            as_ += [f(a_x2, q, 0), f(a_x2, q, 1)]
        as_ += [a_k]
        return b_first, bs, a_first, as_

    def weave(*lists):
        keyed = []
        for n, items in enumerate(lists):
            keyed += [((k + 0.5) / len(items), n, k, item) for k, item in enumerate(items)]
        return [e[3] for e in sorted(keyed, key=lambda e: e[:3])]

    def swap(name, src, dst, dev, moves):
        cp = make(name, src, dst, dev)

        @pl.when(moves)
        def _():
            cp.start()

        @pl.when(jnp.logical_not(moves))
        def _():
            keep = pltpu.make_async_copy(src, dst, lsem.at[2])
            keep.start()
            keep.wait()

    def swapped(name, moves):
        @pl.when(moves)
        def _():
            got(name)

    def part(ref, h):
        return ref.at[pl.ds(h * HALF, HALF), :]

    f = functools.partial

    prepare()
    load_w.wait()
    window_out()
    a1[c] = hat[...].astype(BF16)
    own[0] = hbt[...].astype(BF16)
    pl.semaphore_wait(bar, 8 + jnp.where(c != 0, 1, 0) + jnp.where(r != 0, 1, 0))
    for h in (0, 1):
        swap(("s1", h), part(own.at[0], h), part(mid_sw.at[0], h), (rc, c), c != 0)
    b_first, bs, a_first, as_ = gather_steps(0, a1, b1, lambda col: col, lambda row: xor(row, c))
    a_first(0)
    a_first(1)
    load_p.wait()

    def relay1(h):
        swapped(("s1", h), c != 0)
        swap(("s2", h), part(mid_sw.at[0], h), half(b1, c, h), (r, rc), r != 0)

    def begin1(h):
        swapped(("s2", h), r != 0)
        b_first(h)

    gates = [f(gate_rows, 8 * t, 8 * t + 8, 0) for t in range(16)]
    for step in weave([f(relay1, 0), f(relay1, 1)], gates[:3]):
        step()
    for step in weave([f(begin1, 0), f(begin1, 1)], as_[:4], gates[3:7]):
        step()
    for step in weave(bs, as_[4:], gates[7:]):
        step()

    product(a1, b1, 0, 64)
    finish(0, 1, 0)
    window_in()
    own[1] = hat[...].astype(BF16)
    b2[r] = hbt[...].astype(BF16)
    b_first, bs, a_first, as_ = gather_steps(1, a2, b2, lambda col: xor(r, col), lambda row: row)
    for h in (0, 1):
        swap(("t1", h), part(own.at[1], h), part(mid_sw.at[1], h), (r, rc), r != 0)
    b_first(0)
    b_first(1)

    def relay2(h):
        swapped(("t1", h), r != 0)
        swap(("t2", h), part(mid_sw.at[1], h), half(a2, r, h), (rc, c), c != 0)

    def begin2(h):
        swapped(("t2", h), c != 0)
        a_first(h)

    rest = []
    for t in range(1, 16):
        rest.append(f(finish, t, t + 1, 0))
    gates = [f(gate_rows, 8 * t, 8 * t + 8, 1) for t in range(16)]
    work = rest + gates
    for step in weave([f(relay2, 0), f(relay2, 1)], work[:4]):
        step()
    for step in weave([f(begin2, 0), f(begin2, 1)], bs[:2], work[4:8]):
        step()
    for step in weave(bs[2:], as_, work[8:]):
        step()

    product(a2, b2, 0, 64)
    outs = []
    for t in range(4):
        finish(4 * t, 4 * t + 4, 1)
        rows = pl.ds(32 * t, 32)
        cp = pltpu.make_async_copy(pairv.at[rows], out_ref.at[rows], lsem.at[3 + t])
        cp.start()
        outs.append(cp)
    guard = {"s1": c != 0, "s2": r != 0, "t1": r != 0, "t2": c != 0}
    for name, cp in copies.items():
        if name[0] in guard:
            pl.when(guard[name[0]])(cp.wait_send)
        else:
            cp.wait_send()
    for cp in outs:
        cp.wait()


def per_device(pair, mask, in_gain, in_bias, proj, gate_w, out_gain, out_bias, out_w):
    vm = pl.BlockSpec(memory_space=pltpu.VMEM)
    anyspace = pl.BlockSpec(memory_space=pl.ANY)
    cells = N * N * C
    return pl.pallas_call(
        kernel,
        out_shape=jax.ShapeDtypeStruct((N, N, C), BF16),
        in_specs=[anyspace] + [vm] * 8,
        out_specs=anyspace,
        scratch_shapes=[
            pltpu.VMEM((N, 16, C), BF16),
            pltpu.VMEM((N, N, C), BF16),
            pltpu.VMEM((N, N, C), BF16),
            pltpu.VMEM((RING, PIECE, N), BF16),
            pltpu.VMEM((RING, PIECE, N), BF16),
            pltpu.VMEM((RING, PIECE, N), BF16),
            pltpu.VMEM((RING, PIECE, N), BF16),
            pltpu.VMEM((16, 8 * C, N), F32),
            pltpu.VMEM((PIECE, C), F32),
            pltpu.VMEM((PIECE, C), F32),
            pltpu.VMEM((PIECE, N), F32),
            pltpu.VMEM((PIECE, N), F32),
            pltpu.VMEM((2, PIECE, N), BF16),
            pltpu.VMEM((2, PIECE, N), BF16),
            pltpu.VMEM((2, 256, N), BF16),
            pltpu.VMEM((4, C, C), F32),
            pltpu.VMEM((N, N), F32),
            pltpu.SemaphoreType.DMA((SEMS,)),
            pltpu.SemaphoreType.DMA((SEMS,)),
            pltpu.SemaphoreType.DMA((8,)),
        ],
        compiler_params=pltpu.CompilerParams(
            collective_id=0, has_side_effects=True, vmem_limit_bytes=56 * MIB
        ),
        cost_estimate=pl.CostEstimate(
            flops=8 * cells * C, bytes_accessed=4 * cells, transcendentals=2 * cells
        ),
        name="triangle_updates",
    )(pair, mask, in_gain, in_bias, proj, gate_w, out_gain, out_bias, out_w)


def solution(mesh):
    placed = (P("row", "col", None), P("row", "col"), P(), P(), P(), P(), P(), P(), P())
    return jax.shard_map(
        per_device, mesh=mesh, in_specs=placed, out_specs=P("row", "col", None), check_vma=False
    )
```

```python
import functools

import jax
import jax.numpy as jnp
from jax import lax
from jax.experimental import pallas as pl
from jax.experimental.pallas import tpu as pltpu
from jax.sharding import PartitionSpec as P

C = 128
N = 128
WIN = 8
RING = 16
PIECE = C * WIN
HALF = PIECE // 2
EPS = 1e-5
GATE = 4
UNROLL = 4
MIB = 1024 * 1024
SEMS = 160
F32 = jnp.float32
BF16 = jnp.bfloat16


def xor(a, b):
    total = 0
    for bit in (1, 2, 4, 8):
        total = total + lax.rem(lax.div(a, bit) + lax.div(b, bit), 2) * bit
    return total


def flip(a):
    low, next_ = lax.rem(a, 2), lax.rem(lax.div(a, 2), 2)
    return a - low - 2 * next_ + 2 * low + next_


def sigmoid(z):
    return 0.5 * jnp.tanh(0.5 * z) + 0.5


def norm_lanes(x, gain, bias):
    centre = jnp.mean(x, -1, keepdims=True)
    s = x - centre
    var = jnp.mean(s * s, -1, keepdims=True)
    return s * lax.rsqrt(var + EPS) * gain + bias


def kernel(
    pair_ref, mask_ref, ing_ref, inb_ref, pw_ref, gw_ref, outg_ref, outb_ref, ow_ref, out_ref,
    wbuf, pairv, gate, a1, b1, a2, b2, xs, ha, hb, hat, hbt, own, mid_sw, parity, mean_w, cols, maskt,
    ssem, rsem, lsem,
):
    r = lax.axis_index("row")
    c = lax.axis_index("col")
    y, zh = lax.div(r, 4), lax.rem(r, 4)
    zl, x, core = lax.div(c, 8), lax.rem(lax.div(c, 2), 4), lax.rem(c, 2)
    via_row = xor(r, flip(c))
    via_col = flip(xor(r, c))

    to_col = xor(r, flip(c))

    def row_at(dz, dy):
        return lax.rem(y + dy + 4, 4) * 4 + lax.rem(zh + dz + 4, 4)

    def col_at(dl, dx):
        return lax.rem(zl + dl, 2) * 8 + lax.rem(x + dx + 4, 4) * 2 + core

    sibling = c + 1 - 2 * core

    load_w = pltpu.make_async_copy(pair_ref.at[:, pl.ds(0, 16), :], wbuf, lsem.at[0])
    load_w.start()
    load_p = pltpu.make_async_copy(pair_ref, pairv, lsem.at[1])
    load_p.start()

    bar = pltpu.get_barrier_semaphore()

    def greet(dev):
        pl.semaphore_signal(bar, inc=1, device_id=dev, device_id_type=pl.DeviceIdType.MESH)

    fixed = [
        (row_at(0, 1), c), (row_at(0, -1), c), (row_at(1, 0), c), (row_at(-1, 0), c),
        (r, col_at(0, 1)), (r, col_at(0, -1)), (r, col_at(1, 0)), (r, sibling),
    ]
    for dev in fixed:
        greet(dev)

    @pl.when(c != 0)
    def _():
        greet((via_row, c))

    @pl.when(to_col != c)
    def _():
        greet((r, to_col))
        greet((r, via_col))

    copies = {}

    def make(name, src, dst, dev):
        n = len(copies)
        cp = pltpu.make_async_remote_copy(
            src_ref=src, dst_ref=dst, send_sem=ssem.at[n], recv_sem=rsem.at[n],
            device_id=dev, device_id_type=pl.DeviceIdType.MESH,
        )
        copies[name] = cp
        return cp

    def post(name, src, dst, dev):
        make(name, src, dst, dev).start()

    def got(name):
        copies[name].wait_recv()

    def half(ref, slot, h):
        return ref.at[slot, pl.ds(h * HALF, HALF), :]

    def prepare():
        row = lax.broadcasted_iota(jnp.int32, (256, N), 0)
        low = lax.rem(row, 16) < 8
        parity[0] = jnp.where(low, 1.0, 0.0).astype(BF16)
        parity[1] = jnp.where(low, 0.0, 1.0).astype(BF16)
        mean_w[...] = jnp.full((C, C), 1.0 / C, BF16)
        for d in range(2):
            cols[2 * d] = jnp.broadcast_to(outg_ref[pl.ds(d, 1), :], (C, C)).T
            cols[2 * d + 1] = jnp.broadcast_to(outb_ref[pl.ds(d, 1), :], (C, C)).T
        maskt[...] = mask_ref[...].astype(F32).T

    def project(n, d, store):
        h = jnp.dot(n, pw_ref[d], preferred_element_type=F32)
        store(ha, sigmoid(h[:, :C]) * h[:, C : 2 * C])
        store(hb, sigmoid(h[:, 2 * C : 3 * C]) * h[:, 3 * C :])

    def window_out():
        g, b = ing_ref[pl.ds(0, 1), :], inb_ref[pl.ds(0, 1), :]

        def body(t, carry):
            v = wbuf[pl.ds(t * 16, 16)].astype(F32)[:, :WIN, :].reshape(16 * WIN, C)
            n = norm_lanes(v, g, b).astype(BF16)

            def store(ref, val):
                ref[pl.ds(pl.multiple_of(t * 128, 128), 128), :] = val

            project(n, 0, store)
            return carry

        lax.fori_loop(0, 8, body, 0)
        for src, dst in ((ha, hat), (hb, hbt)):
            for k in range(WIN):
                t = src[pl.ds(k, N, stride=WIN), :].T
                dst[pl.ds(k, C, stride=WIN), :] = t * maskt[pl.ds(k, 1), :]

    def window_in():
        g, b = ing_ref[pl.ds(1, 1), :], inb_ref[pl.ds(1, 1), :]
        for k in range(WIN):
            v = pairv[k].astype(F32)
            n = norm_lanes(v, g, b).astype(BF16)
            m = mask_ref[pl.ds(k, 1), :].astype(F32)
            h = jnp.dot(n, pw_ref[1], preferred_element_type=F32)
            av = sigmoid(h[:, :C]) * h[:, C : 2 * C]
            bv = sigmoid(h[:, 2 * C : 3 * C]) * h[:, 3 * C :]
            hat[pl.ds(k, C, stride=WIN), :] = av.T * m
            hbt[pl.ds(k, C, stride=WIN), :] = bv.T * m

    def gate_rows(lo, hi, d):
        g, b = ing_ref[pl.ds(d, 1), :], inb_ref[pl.ds(d, 1), :]

        def body(t, carry):
            v = pairv[pl.ds(t * GATE, GATE)].reshape(GATE * N, C)
            s = v.astype(F32) - jnp.dot(v, mean_w[...], preferred_element_type=F32)
            var = jnp.dot((s * s).astype(BF16), mean_w[...], preferred_element_type=F32)
            n = (s * lax.rsqrt(var + EPS) * g + b).astype(BF16)
            z = jnp.dot(n, gw_ref[d], preferred_element_type=F32)
            gate[pl.ds(t * GATE, GATE)] = sigmoid(z).astype(BF16).reshape(GATE, N, C)
            return carry

        lax.fori_loop(lo // GATE, hi // GATE, body, 0)

    def product(a, b, lo, hi):
        def one(t):
            rows = pl.ds(pl.multiple_of(t * 16, 16), 16)
            lhs = a[:, rows, :].reshape(256, N)
            rhs = b[:, rows, :].reshape(256, N)
            both = jnp.concatenate([rhs * parity[0], rhs * parity[1]], axis=1)
            out = lax.dot_general(lhs, both, (((0,), (0,)), ((), ())), preferred_element_type=F32)
            base = pl.multiple_of(t * 16, 16)
            xs[:, pl.ds(base, 8), :] = out[:, :N].reshape(16, 8, N)
            xs[:, pl.ds(base + 8, 8), :] = out[:, N:].reshape(16, 8, N)

        def body(t, carry):
            for k in range(UNROLL):
                one(t * UNROLL + k)
            return carry

        lax.fori_loop(lo // UNROLL, hi // UNROLL, body, 0)

    def finish(lo, hi, d):
        def body(t, carry):
            for i8 in range(8):
                v = xs[t, pl.ds(i8, C, stride=8), :]
                centre = jnp.mean(v, 0, keepdims=True)
                s = v - centre
                var = jnp.mean(s * s, 0, keepdims=True)
                n = s * lax.rsqrt(var + EPS) * cols[2 * d] + cols[2 * d + 1]
                u = lax.dot_general(
                    n.astype(BF16), ow_ref[d], (((0,), (0,)), ((), ())), preferred_element_type=F32
                )
                i = t * 8 + i8
                old = pairv[i].astype(F32)
                pairv[i] = (old + gate[i].astype(F32) * u).astype(BF16)
            return carry

        lax.fori_loop(lo, hi, body, 0)

    def gather_steps(p, a, b, lab_a, lab_b):
        steps = []

        def b_first_z(h):
            s = half(b, lab_b(r), h)
            for dz in (1, -1):
                post((p, "z", dz, h), s, s, (row_at(dz, 0), c))

        def b_first_y(h):
            s = half(b, lab_b(r), h)
            for dy in (1, -1):
                post((p, "y", 0, dy, h), s, s, (row_at(0, dy), c))

        def b_z(dz, h):
            got((p, "z", dz, h))
            s = half(b, lab_b(row_at(-dz, 0)), h)
            if (dz == 1) == (h == 0):
                post((p, "z", 2, h), s, s, (row_at(dz, 0), c))
            for dy in (1, -1):
                post((p, "y", -dz, dy, h), s, s, (row_at(0, dy), c))

        def b_z2(h):
            got((p, "z", 2, h))
            s = half(b, lab_b(row_at(2, 0)), h)
            for dy in (1, -1):
                post((p, "y", 2, dy, h), s, s, (row_at(0, dy), c))

        def b_y(q, dy, h):
            got((p, "y", q, dy, h))
            if (dy == 1) == (h == 0):
                s = half(b, lab_b(row_at(q, -dy)), h)
                post((p, "y2", q, h), s, s, (row_at(0, dy), c))

        def b_y2(q, h):
            got((p, "y2", q, h))

        def a_first(h):
            s = half(a, lab_a(c), h)
            post((p, "l", h), s, s, (r, col_at(1, 0)))
            for dx in (1, -1):
                post((p, "x", 0, dx, h), s, s, (r, col_at(0, dx)))
            post((p, "k", 0, 0, h), s, s, (r, sibling))

        def a_l(h):
            got((p, "l", h))
            s = half(a, lab_a(col_at(1, 0)), h)
            for dx in (1, -1):
                post((p, "x", 1, dx, h), s, s, (r, col_at(0, dx)))
            post((p, "k", 1, 0, h), s, s, (r, sibling))

        def a_x(q, dx, h):
            got((p, "x", q, dx, h))
            s = half(a, lab_a(col_at(q, -dx)), h)
            if (dx == 1) == (h == 0):
                post((p, "x2", q, h), s, s, (r, col_at(0, dx)))
            post((p, "k", q, -dx, h), s, s, (r, sibling))

        def a_x2(q, h):
            got((p, "x2", q, h))
            s = half(a, lab_a(col_at(q, 2)), h)
            post((p, "k", q, 2, h), s, s, (r, sibling))

        def a_k():
            for q in (0, 1):
                for dx in (0, 1, -1, 2):
                    for h in (0, 1):
                        got((p, "k", q, dx, h))

        f = functools.partial
        zs = [f(b_z, 1, 0), f(b_z, -1, 0), f(b_z, 1, 1), f(b_z, -1, 1)]
        bs = []
        for h in (0, 1):
            bs += [f(b_y, 0, 1, h), f(b_y, 0, -1, h)]
        bs += [f(b_z2, 0), f(b_z2, 1)]
        for h in (0, 1):
            for q in (1, -1):
                bs += [f(b_y, q, 1, h), f(b_y, q, -1, h)]
        bs += [f(b_y2, 0, 0), f(b_y2, 0, 1)]
        for h in (0, 1):
            bs += [f(b_y, 2, 1, h), f(b_y, 2, -1, h)]
        for q in (1, -1, 2):
            bs += [f(b_y2, q, 0), f(b_y2, q, 1)]
        as_ = [f(a_l, 0), f(a_l, 1)]
        for q in (0, 1):
            for h in (0, 1):
                as_ += [f(a_x, q, 1, h), f(a_x, q, -1, h)]
        for q in (0, 1):
            as_ += [f(a_x2, q, 0), f(a_x2, q, 1)]
        as_ += [a_k]
        return b_first_z, b_first_y, zs, bs, a_first, as_

    def weave(*lists, late=(0.0, 0.0, 0.0)):
        keyed = []
        for n, items in enumerate(lists):
            for k, item in enumerate(items):
                at = late[n] + (1.0 - late[n]) * (k + 0.5) / len(items)
                keyed.append((at, n, k, item))
        return [e[3] for e in sorted(keyed, key=lambda e: e[:3])]

    def swap(name, src, dst, dev, moves):
        cp = make(name, src, dst, dev)

        @pl.when(moves)
        def _():
            cp.start()

        @pl.when(jnp.logical_not(moves))
        def _():
            keep = pltpu.make_async_copy(src, dst, lsem.at[2])
            keep.start()
            keep.wait()

    def swapped(name, moves):
        @pl.when(moves)
        def _():
            got(name)

    def part(ref, h):
        return ref.at[pl.ds(h * HALF, HALF), :]

    f = functools.partial

    prepare()
    load_w.wait()
    window_out()
    a1[c] = hat[...].astype(BF16)
    own[0] = hbt[...].astype(BF16)
    pl.semaphore_wait(bar, 8 + jnp.where(c != 0, 1, 0) + jnp.where(to_col != c, 2, 0))
    def swap1(h):
        swap(("s1", h), part(own.at[0], h), part(mid_sw.at[0], h), (via_row, c), c != 0)

    def relay1(h):
        swapped(("s1", h), c != 0)
        swap(("s2", h), part(mid_sw.at[0], h), half(b1, c, h), (r, to_col), to_col != c)

    swap1(0)
    bz, by, zs, bs, a_first, as_ = gather_steps(
        0, a1, b1, lambda col: col, lambda row: flip(xor(row, c))
    )
    load_p.wait()
    gates = [f(gate_rows, 8 * t, 8 * t + 8, 0) for t in range(16)]
    gates[0]()
    relay1(0)
    swap1(1)
    gates[1]()
    relay1(1)
    swapped(("s2", 0), to_col != c)
    bz(0)
    by(0)
    a_first(0)
    gates[2]()
    swapped(("s2", 1), to_col != c)
    by(1)
    zs[0]()
    zs[1]()
    bz(1)
    a_first(1)
    for step in weave(bs[:2] + zs[2:] + bs[2:], as_, gates[3:], late=(0.0, 0.2, 0.0)):
        step()

    product(a1, b1, 0, 64)
    finish(0, 1, 0)
    window_in()
    own[1] = hat[...].astype(BF16)
    b2[r] = hbt[...].astype(BF16)
    bz, by, zs, bs, a_first, as_ = gather_steps(
        1, a2, b2, lambda col: xor(r, flip(col)), lambda row: row
    )

    def swap2(h):
        swap(("t1", h), part(own.at[1], h), part(mid_sw.at[1], h), (r, via_col), to_col != c)

    def relay2(h):
        swapped(("t1", h), to_col != c)
        swap(("t2", h), part(mid_sw.at[1], h), half(a2, r, h), (via_row, c), c != 0)

    def begin2(h):
        swapped(("t2", h), c != 0)
        a_first(h)

    swap2(0)
    bz(0)
    by(0)
    by(1)
    work = [f(finish, t, t + 1, 0) for t in range(1, 16)]
    work += [f(gate_rows, 8 * t, 8 * t + 8, 1) for t in range(16)]
    for step in work[:5]:
        step()
    relay2(0)
    swap2(1)
    zs[0]()
    zs[1]()
    bz(1)
    for step in work[5:8]:
        step()
    relay2(1)
    begin2(0)
    for step in bs[:2] + work[8:10] + zs[2:] + bs[2:4] + [f(begin2, 1)]:
        step()
    for step in weave(bs[4:], as_, work[10:]):
        step()

    product(a2, b2, 0, 64)
    outs = []
    for t in range(4):
        finish(4 * t, 4 * t + 4, 1)
        rows = pl.ds(32 * t, 32)
        cp = pltpu.make_async_copy(pairv.at[rows], out_ref.at[rows], lsem.at[3 + t])
        cp.start()
        outs.append(cp)
    guard = {"s1": c != 0, "s2": to_col != c, "t1": to_col != c, "t2": c != 0}
    for name, cp in copies.items():
        if name[0] in guard:
            pl.when(guard[name[0]])(cp.wait_send)
        else:
            cp.wait_send()
    for cp in outs:
        cp.wait()


def per_device(pair, mask, in_gain, in_bias, proj, gate_w, out_gain, out_bias, out_w):
    vm = pl.BlockSpec(memory_space=pltpu.VMEM)
    anyspace = pl.BlockSpec(memory_space=pl.ANY)
    cells = N * N * C
    return pl.pallas_call(
        kernel,
        out_shape=jax.ShapeDtypeStruct((N, N, C), BF16),
        in_specs=[anyspace] + [vm] * 8,
        out_specs=anyspace,
        scratch_shapes=[
            pltpu.VMEM((N, 16, C), BF16),
            pltpu.VMEM((N, N, C), BF16),
            pltpu.VMEM((N, N, C), BF16),
            pltpu.VMEM((RING, PIECE, N), BF16),
            pltpu.VMEM((RING, PIECE, N), BF16),
            pltpu.VMEM((RING, PIECE, N), BF16),
            pltpu.VMEM((RING, PIECE, N), BF16),
            pltpu.VMEM((16, 8 * C, N), F32),
            pltpu.VMEM((PIECE, C), F32),
            pltpu.VMEM((PIECE, C), F32),
            pltpu.VMEM((PIECE, N), F32),
            pltpu.VMEM((PIECE, N), F32),
            pltpu.VMEM((2, PIECE, N), BF16),
            pltpu.VMEM((2, PIECE, N), BF16),
            pltpu.VMEM((2, 256, N), BF16),
            pltpu.VMEM((C, C), BF16),
            pltpu.VMEM((4, C, C), F32),
            pltpu.VMEM((N, N), F32),
            pltpu.SemaphoreType.DMA((SEMS,)),
            pltpu.SemaphoreType.DMA((SEMS,)),
            pltpu.SemaphoreType.DMA((8,)),
        ],
        compiler_params=pltpu.CompilerParams(
            collective_id=0, has_side_effects=True, vmem_limit_bytes=56 * MIB
        ),
        cost_estimate=pl.CostEstimate(
            flops=8 * cells * C, bytes_accessed=4 * cells, transcendentals=2 * cells
        ),
        name="triangle_updates",
    )(pair, mask, in_gain, in_bias, proj, gate_w, out_gain, out_bias, out_w)


def solution(mesh):
    placed = (P("row", "col", None), P("row", "col"), P(), P(), P(), P(), P(), P(), P())
    return jax.shard_map(
        per_device, mesh=mesh, in_specs=placed, out_specs=P("row", "col", None), check_vma=False
    )
```

```python
import functools

import jax
import jax.numpy as jnp
from jax import lax
from jax.experimental import pallas as pl
from jax.experimental.pallas import tpu as pltpu
from jax.sharding import PartitionSpec as P

C = 128
N = 128
WIN = 8
RING = 16
PIECE = C * WIN
HALF = PIECE // 2
EPS = 1e-5
GATE = 4
UNROLL = 8
MIB = 1024 * 1024
SEMS = 160
F32 = jnp.float32
BF16 = jnp.bfloat16


def xor(a, b):
    total = 0
    for bit in (1, 2, 4, 8):
        total = total + lax.rem(lax.div(a, bit) + lax.div(b, bit), 2) * bit
    return total


def flip(a):
    low, next_ = lax.rem(a, 2), lax.rem(lax.div(a, 2), 2)
    return a - low - 2 * next_ + 2 * low + next_


def sigmoid(z):
    return 0.5 * jnp.tanh(0.5 * z) + 0.5


def norm_lanes(x, gain, bias):
    centre = jnp.mean(x, -1, keepdims=True)
    s = x - centre
    var = jnp.mean(s * s, -1, keepdims=True)
    return s * lax.rsqrt(var + EPS) * gain + bias


def kernel(
    pair_ref, mask_ref, ing_ref, inb_ref, pw_ref, gw_ref, outg_ref, outb_ref, ow_ref, out_ref,
    wbuf, pairv, gate, a1, b1, a2, b2, xs, ha, hb, hat, hbt, own, mid_sw, parity, mean_w, cols, maskt,
    ssem, rsem, lsem,
):
    r = lax.axis_index("row")
    c = lax.axis_index("col")
    y, zh = lax.div(r, 4), lax.rem(r, 4)
    zl, x, core = lax.div(c, 8), lax.rem(lax.div(c, 2), 4), lax.rem(c, 2)
    via_row = xor(r, flip(c))
    via_col = flip(xor(r, c))

    to_col = xor(r, flip(c))

    def row_at(dz, dy):
        return lax.rem(y + dy + 4, 4) * 4 + lax.rem(zh + dz + 4, 4)

    def col_at(dl, dx):
        return lax.rem(zl + dl, 2) * 8 + lax.rem(x + dx + 4, 4) * 2 + core

    sibling = c + 1 - 2 * core

    load_w = pltpu.make_async_copy(pair_ref.at[:, pl.ds(0, 16), :], wbuf, lsem.at[0])
    load_w.start()
    load_p = pltpu.make_async_copy(pair_ref, pairv, lsem.at[1])
    load_p.start()

    bar = pltpu.get_barrier_semaphore()

    def greet(dev):
        pl.semaphore_signal(bar, inc=1, device_id=dev, device_id_type=pl.DeviceIdType.MESH)

    fixed = [
        (row_at(0, 1), c), (row_at(0, -1), c), (row_at(1, 0), c), (row_at(-1, 0), c),
        (r, col_at(0, 1)), (r, col_at(0, -1)), (r, col_at(1, 0)), (r, sibling),
    ]
    for dev in fixed:
        greet(dev)

    @pl.when(c != 0)
    def _():
        greet((via_row, c))

    @pl.when(to_col != c)
    def _():
        greet((r, to_col))
        greet((r, via_col))

    copies = {}

    def make(name, src, dst, dev):
        n = len(copies)
        cp = pltpu.make_async_remote_copy(
            src_ref=src, dst_ref=dst, send_sem=ssem.at[n], recv_sem=rsem.at[n],
            device_id=dev, device_id_type=pl.DeviceIdType.MESH,
        )
        copies[name] = cp
        return cp

    def post(name, src, dst, dev):
        make(name, src, dst, dev).start()

    def got(name):
        copies[name].wait_recv()

    def half(ref, slot, h):
        return ref.at[slot, pl.ds(h * HALF, HALF), :]

    def prepare():
        row = lax.broadcasted_iota(jnp.int32, (256, N), 0)
        low = lax.rem(row, 16) < 8
        parity[0] = jnp.where(low, 1.0, 0.0).astype(BF16)
        parity[1] = jnp.where(low, 0.0, 1.0).astype(BF16)
        mean_w[...] = jnp.full((C, C), 1.0 / C, BF16)
        for d in range(2):
            cols[2 * d] = jnp.broadcast_to(outg_ref[pl.ds(d, 1), :], (C, C)).T
            cols[2 * d + 1] = jnp.broadcast_to(outb_ref[pl.ds(d, 1), :], (C, C)).T
        maskt[...] = mask_ref[...].astype(F32).T

    def project(n, d, store):
        h = jnp.dot(n, pw_ref[d], preferred_element_type=F32)
        store(ha, sigmoid(h[:, :C]) * h[:, C : 2 * C])
        store(hb, sigmoid(h[:, 2 * C : 3 * C]) * h[:, 3 * C :])

    def window_out():
        g, b = ing_ref[pl.ds(0, 1), :], inb_ref[pl.ds(0, 1), :]

        def body(t, carry):
            v = wbuf[pl.ds(t * 16, 16)].astype(F32)[:, :WIN, :].reshape(16 * WIN, C)
            n = norm_lanes(v, g, b).astype(BF16)

            def store(ref, val):
                ref[pl.ds(pl.multiple_of(t * 128, 128), 128), :] = val

            project(n, 0, store)
            return carry

        lax.fori_loop(0, 8, body, 0)
        for src, dst in ((ha, hat), (hb, hbt)):
            for k in range(WIN):
                t = src[pl.ds(k, N, stride=WIN), :].T
                dst[pl.ds(k, C, stride=WIN), :] = t * maskt[pl.ds(k, 1), :]

    def window_in():
        g, b = ing_ref[pl.ds(1, 1), :], inb_ref[pl.ds(1, 1), :]
        for k in range(WIN):
            v = pairv[k].astype(F32)
            n = norm_lanes(v, g, b).astype(BF16)
            m = mask_ref[pl.ds(k, 1), :].astype(F32)
            h = jnp.dot(n, pw_ref[1], preferred_element_type=F32)
            av = sigmoid(h[:, :C]) * h[:, C : 2 * C]
            bv = sigmoid(h[:, 2 * C : 3 * C]) * h[:, 3 * C :]
            hat[pl.ds(k, C, stride=WIN), :] = av.T * m
            hbt[pl.ds(k, C, stride=WIN), :] = bv.T * m

    def gate_rows(lo, hi, d):
        g, b = ing_ref[pl.ds(d, 1), :], inb_ref[pl.ds(d, 1), :]

        def body(t, carry):
            v = pairv[pl.ds(t * GATE, GATE)].reshape(GATE * N, C)
            s = v.astype(F32) - jnp.dot(v, mean_w[...], preferred_element_type=F32)
            var = jnp.dot((s * s).astype(BF16), mean_w[...], preferred_element_type=F32)
            n = (s * lax.rsqrt(var + EPS) * g + b).astype(BF16)
            z = jnp.dot(n, gw_ref[d], preferred_element_type=F32)
            gate[pl.ds(t * GATE, GATE)] = sigmoid(z).astype(BF16).reshape(GATE, N, C)
            return carry

        lax.fori_loop(lo // GATE, hi // GATE, body, 0)

    def product(a, b, lo, hi):
        def one(t):
            rows = pl.ds(pl.multiple_of(t * 16, 16), 16)
            lhs = a[:, rows, :].reshape(256, N)
            rhs = b[:, rows, :].reshape(256, N)
            both = jnp.concatenate([rhs * parity[0], rhs * parity[1]], axis=1)
            out = lax.dot_general(lhs, both, (((0,), (0,)), ((), ())), preferred_element_type=F32)
            base = pl.multiple_of(t * 16, 16)
            xs[:, pl.ds(base, 8), :] = out[:, :N].reshape(16, 8, N)
            xs[:, pl.ds(base + 8, 8), :] = out[:, N:].reshape(16, 8, N)

        def body(t, carry):
            for k in range(UNROLL):
                one(t * UNROLL + k)
            return carry

        lax.fori_loop(lo // UNROLL, hi // UNROLL, body, 0)

    def finish(lo, hi, d):
        def body(t, carry):
            for i8 in range(8):
                v = xs[t, pl.ds(i8, C, stride=8), :]
                centre = jnp.mean(v, 0, keepdims=True)
                s = v - centre
                var = jnp.mean(s * s, 0, keepdims=True)
                n = s * lax.rsqrt(var + EPS) * cols[2 * d] + cols[2 * d + 1]
                u = lax.dot_general(
                    n.astype(BF16), ow_ref[d], (((0,), (0,)), ((), ())), preferred_element_type=F32
                )
                i = t * 8 + i8
                old = pairv[i].astype(F32)
                pairv[i] = (old + gate[i].astype(F32) * u).astype(BF16)
            return carry

        lax.fori_loop(lo, hi, body, 0)

    def gather_steps(p, a, b, lab_a, lab_b):
        steps = []

        def b_first_z(h):
            s = half(b, lab_b(r), h)
            for dz in (1, -1):
                post((p, "z", dz, h), s, s, (row_at(dz, 0), c))

        def b_first_y(h):
            s = half(b, lab_b(r), h)
            for dy in (1, -1):
                post((p, "y", 0, dy, h), s, s, (row_at(0, dy), c))

        def b_z(dz, h):
            got((p, "z", dz, h))
            s = half(b, lab_b(row_at(-dz, 0)), h)
            if (dz == 1) == (h == 0):
                post((p, "z", 2, h), s, s, (row_at(dz, 0), c))
            for dy in (1, -1):
                post((p, "y", -dz, dy, h), s, s, (row_at(0, dy), c))

        def b_z2(h):
            got((p, "z", 2, h))
            s = half(b, lab_b(row_at(2, 0)), h)
            for dy in (1, -1):
                post((p, "y", 2, dy, h), s, s, (row_at(0, dy), c))

        def b_y(q, dy, h):
            got((p, "y", q, dy, h))
            if (dy == 1) == (h == 0):
                s = half(b, lab_b(row_at(q, -dy)), h)
                post((p, "y2", q, h), s, s, (row_at(0, dy), c))

        def b_y2(q, h):
            got((p, "y2", q, h))

        def a_first(h):
            s = half(a, lab_a(c), h)
            post((p, "l", h), s, s, (r, col_at(1, 0)))
            for dx in (1, -1):
                post((p, "x", 0, dx, h), s, s, (r, col_at(0, dx)))
            post((p, "k", 0, 0, h), s, s, (r, sibling))

        def a_l(h):
            got((p, "l", h))
            s = half(a, lab_a(col_at(1, 0)), h)
            for dx in (1, -1):
                post((p, "x", 1, dx, h), s, s, (r, col_at(0, dx)))
            post((p, "k", 1, 0, h), s, s, (r, sibling))

        def a_x(q, dx, h):
            got((p, "x", q, dx, h))
            s = half(a, lab_a(col_at(q, -dx)), h)
            if (dx == 1) == (h == 0):
                post((p, "x2", q, h), s, s, (r, col_at(0, dx)))
            post((p, "k", q, -dx, h), s, s, (r, sibling))

        def a_x2(q, h):
            got((p, "x2", q, h))
            s = half(a, lab_a(col_at(q, 2)), h)
            post((p, "k", q, 2, h), s, s, (r, sibling))

        def a_k():
            for q in (0, 1):
                for dx in (0, 1, -1, 2):
                    for h in (0, 1):
                        got((p, "k", q, dx, h))

        f = functools.partial
        zs = [f(b_z, 1, 0), f(b_z, -1, 0), f(b_z, 1, 1), f(b_z, -1, 1)]
        bs = []
        for h in (0, 1):
            bs += [f(b_y, 0, 1, h), f(b_y, 0, -1, h)]
        bs += [f(b_z2, 0), f(b_z2, 1)]
        for h in (0, 1):
            for q in (1, -1):
                bs += [f(b_y, q, 1, h), f(b_y, q, -1, h)]
        bs += [f(b_y2, 0, 0), f(b_y2, 0, 1)]
        for h in (0, 1):
            bs += [f(b_y, 2, 1, h), f(b_y, 2, -1, h)]
        for q in (1, -1, 2):
            bs += [f(b_y2, q, 0), f(b_y2, q, 1)]
        as_ = [f(a_l, 0), f(a_l, 1)]
        for q in (0, 1):
            for h in (0, 1):
                as_ += [f(a_x, q, 1, h), f(a_x, q, -1, h)]
        for q in (0, 1):
            as_ += [f(a_x2, q, 0), f(a_x2, q, 1)]
        as_ += [a_k]
        return b_first_z, b_first_y, zs, bs, a_first, as_

    def weave(*lists, late=(0.0, 0.0, 0.0)):
        keyed = []
        for n, items in enumerate(lists):
            for k, item in enumerate(items):
                at = late[n] + (1.0 - late[n]) * (k + 0.5) / len(items)
                keyed.append((at, n, k, item))
        return [e[3] for e in sorted(keyed, key=lambda e: e[:3])]

    def swap(name, src, dst, dev, moves):
        cp = make(name, src, dst, dev)

        @pl.when(moves)
        def _():
            cp.start()

        @pl.when(jnp.logical_not(moves))
        def _():
            keep = pltpu.make_async_copy(src, dst, lsem.at[2])
            keep.start()
            keep.wait()

    def swapped(name, moves):
        @pl.when(moves)
        def _():
            got(name)

    def part(ref, h):
        return ref.at[pl.ds(h * HALF, HALF), :]

    f = functools.partial

    prepare()
    load_w.wait()
    window_out()
    a1[c] = hat[...].astype(BF16)
    own[0] = hbt[...].astype(BF16)
    pl.semaphore_wait(bar, 8 + jnp.where(c != 0, 1, 0) + jnp.where(to_col != c, 2, 0))
    def swap1(h):
        swap(("s1", h), part(own.at[0], h), part(mid_sw.at[0], h), (via_row, c), c != 0)

    def relay1(h):
        swapped(("s1", h), c != 0)
        swap(("s2", h), part(mid_sw.at[0], h), half(b1, c, h), (r, to_col), to_col != c)

    swap1(0)
    bz, by, zs, bs, a_first, as_ = gather_steps(
        0, a1, b1, lambda col: col, lambda row: flip(xor(row, c))
    )
    load_p.wait()
    gates = [f(gate_rows, 8 * t, 8 * t + 8, 0) for t in range(16)]
    gates[0]()
    relay1(0)
    swap1(1)
    gates[1]()
    relay1(1)
    swapped(("s2", 0), to_col != c)
    bz(0)
    by(0)
    a_first(0)
    gates[2]()
    swapped(("s2", 1), to_col != c)
    by(1)
    zs[0]()
    zs[1]()
    bz(1)
    a_first(1)
    for step in weave(bs[:2] + zs[2:] + bs[2:], as_, gates[3:], late=(0.0, 0.2, 0.0)):
        step()

    product(a1, b1, 0, 64)
    finish(0, 1, 0)
    window_in()
    own[1] = hat[...].astype(BF16)
    b2[r] = hbt[...].astype(BF16)
    bz, by, zs, bs, a_first, as_ = gather_steps(
        1, a2, b2, lambda col: xor(r, flip(col)), lambda row: row
    )

    def swap2(h):
        swap(("t1", h), part(own.at[1], h), part(mid_sw.at[1], h), (r, via_col), to_col != c)

    def relay2(h):
        swapped(("t1", h), to_col != c)
        swap(("t2", h), part(mid_sw.at[1], h), half(a2, r, h), (via_row, c), c != 0)

    def begin2(h):
        swapped(("t2", h), c != 0)
        a_first(h)

    swap2(0)
    bz(0)
    by(0)
    by(1)
    work = [f(finish, t, t + 1, 0) for t in range(1, 16)]
    work += [f(gate_rows, 8 * t, 8 * t + 8, 1) for t in range(16)]
    for step in work[:5]:
        step()
    relay2(0)
    swap2(1)
    zs[0]()
    zs[1]()
    bz(1)
    for step in work[5:8]:
        step()
    relay2(1)
    begin2(0)
    for step in bs[:2] + work[8:10] + zs[2:] + bs[2:4] + [f(begin2, 1)]:
        step()
    for step in weave(bs[4:], as_, work[10:]):
        step()

    product(a2, b2, 0, 64)
    outs = []
    for t in range(4):
        finish(4 * t, 4 * t + 4, 1)
        rows = pl.ds(32 * t, 32)
        cp = pltpu.make_async_copy(pairv.at[rows], out_ref.at[rows], lsem.at[3 + t])
        cp.start()
        outs.append(cp)
    guard = {"s1": c != 0, "s2": to_col != c, "t1": to_col != c, "t2": c != 0}
    for name, cp in copies.items():
        if name[0] in guard:
            pl.when(guard[name[0]])(cp.wait_send)
        else:
            cp.wait_send()
    for cp in outs:
        cp.wait()


def per_device(pair, mask, in_gain, in_bias, proj, gate_w, out_gain, out_bias, out_w):
    vm = pl.BlockSpec(memory_space=pltpu.VMEM)
    anyspace = pl.BlockSpec(memory_space=pl.ANY)
    cells = N * N * C
    return pl.pallas_call(
        kernel,
        out_shape=jax.ShapeDtypeStruct((N, N, C), BF16),
        in_specs=[anyspace] + [vm] * 8,
        out_specs=anyspace,
        scratch_shapes=[
            pltpu.VMEM((N, 16, C), BF16),
            pltpu.VMEM((N, N, C), BF16),
            pltpu.VMEM((N, N, C), BF16),
            pltpu.VMEM((RING, PIECE, N), BF16),
            pltpu.VMEM((RING, PIECE, N), BF16),
            pltpu.VMEM((RING, PIECE, N), BF16),
            pltpu.VMEM((RING, PIECE, N), BF16),
            pltpu.VMEM((16, 8 * C, N), F32),
            pltpu.VMEM((PIECE, C), F32),
            pltpu.VMEM((PIECE, C), F32),
            pltpu.VMEM((PIECE, N), F32),
            pltpu.VMEM((PIECE, N), F32),
            pltpu.VMEM((2, PIECE, N), BF16),
            pltpu.VMEM((2, PIECE, N), BF16),
            pltpu.VMEM((2, 256, N), BF16),
            pltpu.VMEM((C, C), BF16),
            pltpu.VMEM((4, C, C), F32),
            pltpu.VMEM((N, N), F32),
            pltpu.SemaphoreType.DMA((SEMS,)),
            pltpu.SemaphoreType.DMA((SEMS,)),
            pltpu.SemaphoreType.DMA((8,)),
        ],
        compiler_params=pltpu.CompilerParams(
            collective_id=0, has_side_effects=True, vmem_limit_bytes=56 * MIB
        ),
        cost_estimate=pl.CostEstimate(
            flops=8 * cells * C, bytes_accessed=4 * cells, transcendentals=2 * cells
        ),
        name="triangle_updates",
    )(pair, mask, in_gain, in_bias, proj, gate_w, out_gain, out_bias, out_w)


def solution(mesh):
    placed = (P("row", "col", None), P("row", "col"), P(), P(), P(), P(), P(), P(), P())
    return jax.shard_map(
        per_device, mesh=mesh, in_specs=placed, out_specs=P("row", "col", None), check_vma=False
    )
```
